32 devices in a mesh: tx: 8 (over y, x, core), ty: 4 (over z).
Axes of the slice: x: 2, y: 2, z: 4, core: 2. Of those that a mesh axis runs over, the one named last changes fastest.
Arguments:
- points: float32 [3, 65536], P(None, ('tx', 'ty')), may hold values from 0 to 1
- tree_order: int32 [32, 2048], P(('tx', 'ty')), may hold values from 0 to 2047, each once within a row
- samples: float32 [65536, 128], P(('tx', 'ty')), may hold values from -6 to 6
- near_leaves: int32 [256, 5], P(('tx', 'ty')), may hold values from 0 to 11, as said below
- near_counts: int32 [256], P(('tx', 'ty')), may hold values from 0 to 5, as said below
Outputs:
- leaf_bases: float32 [65536, 128], P(('tx', 'ty'))
- local_bases: float32 [224, 256, 128], P(('tx', 'ty'))
- upper_bases: float32 [160, 256, 128], P(('tx', 'ty'))
- root_factor: float32 [128, 128], replicated
The draws below stay inside these ranges and needn't reach their ends.
Inputs may be any that keep to these rules, and one draw needn't show every extreme that they name: `near_leaves`: for k < near_counts[i], the entry w at [i, k] names the existing leaf (i // 8) * 8 - 2 + w, which is not i; the leaves named in one row are distinct; entries at k >= near_counts[i] are 0. `near_counts`: leaf 0 lists exactly 5 near-field leaves in every draw. `tree_order`: each row is a permutation of the positions of one device's block.
All inputs are finite; a program needn't handle non-finite values.
Results may differ from the reference program's by a relative error of at most 0.0003.
Values sent between devices are 32-bit elements; how exact they have to be, the bound alone decides.
A program may use at most 64 MiB of HBM per device.

```python
import jax
import jax.numpy as jnp
from jax import lax

RANK = 128
LEAF = 256
LEAVES_DEV = 8
HALO = 2
MAXNB = 5
PTS_DEV = 2048
LEAVES = 256
NPTS = 65536
LEVELS = 5
DEVICES = 32


def near_lists(key):
    count_key, order_key = jax.random.split(jax.random.fold_in(key, 7))
    counts = jax.random.randint(count_key, (LEAVES,), 0, MAXNB + 1)
    counts = counts.at[0].set(MAXNB)
    window_width = LEAVES_DEV + 2 * HALO
    leaf_ids = jnp.arange(LEAVES, dtype=jnp.int32)
    device_ids = leaf_ids // LEAVES_DEV
    window = jnp.arange(window_width, dtype=jnp.int32)
    global_ids = device_ids[:, None] * LEAVES_DEV - HALO + window[None, :]
    invalid = (global_ids < 0) | (global_ids >= LEAVES) | (global_ids == leaf_ids[:, None])
    row_keys = jax.random.split(order_key, LEAVES)
    shuffled = jax.vmap(lambda row_key: jax.random.permutation(row_key, window_width))(row_keys)
    scores = shuffled.astype(jnp.int32) + window_width * invalid.astype(jnp.int32)
    chosen = jnp.argsort(scores, axis=1)[:, :MAXNB].astype(jnp.int32)
    filled = jnp.arange(MAXNB, dtype=jnp.int32)[None, :] < counts[:, None]
    return (jnp.where(filled, chosen, 0).astype(jnp.int32), counts.astype(jnp.int32))


def draw_near_leaves(key, part):
    return near_lists(key)[0]


def draw_near_counts(key, part):
    return near_lists(key)[1]


def block_scale(own_key, dims, cuts, low, top_value):
    factor_of, own = 1.0, jax.random.fold_in(own_key, 6)
    for dim, parts in cuts:
        draws = jnp.exp(jax.random.uniform(jax.random.fold_in(own, dim), (parts,), jnp.float32, low / len(cuts), top_value / len(cuts)))
        factor_of = factor_of * jnp.repeat(draws, dims[dim] // parts).reshape([-1 if axis == dim else 1 for axis in range(len(dims))])
    return factor_of


def normal_values(key, shape, deviation, limit, pieces=(), kind=jnp.bfloat16):
    factor_of = block_scale(key, shape, pieces, -0.22, 0.18) if pieces else 1.0
    array = jax.random.normal(key, shape, jnp.float32) * deviation * factor_of
    return jnp.minimum(jnp.maximum(array, -limit), limit).astype(kind)


def setup_inputs(seed: int = 0) -> dict:
    splits = jax.random.split(jax.random.key(seed), 6)
    points = jnp.clip(1.0 * jax.random.uniform(splits[0], (3, NPTS), jnp.float32) ** block_scale(splits[0], (3, NPTS), ((1, 32),), -0.2, 0.2), 0.0, 1.0)
    tree_order = jax.vmap(lambda own: jax.random.permutation(own, PTS_DEV))(jax.random.split(splits[1], DEVICES)).reshape((DEVICES, PTS_DEV)).astype(jnp.int32)
    samples = normal_values(splits[2], (NPTS, RANK), 1.0, 6.0, ((0, 32),), jnp.float32)
    near_leaves = draw_near_leaves(jax.random.fold_in(splits[5], 71), 0)
    near_counts = draw_near_counts(jax.random.fold_in(splits[5], 71), 0)
    return {"points": points, "tree_order": tree_order, "samples": samples, "near_leaves": near_leaves, "near_counts": near_counts}


SPREAD = 50.0

def orthonormalize(stacked):
    gram_matrix = jnp.einsum('...ir,...is->...rs', stacked, stacked, precision=lax.Precision.HIGHEST)
    lower_factor = jnp.linalg.cholesky(gram_matrix)
    basis_rows = jax.scipy.linalg.solve_triangular(lower_factor, jnp.swapaxes(stacked, -1, -2), lower=True)
    return (jnp.swapaxes(basis_rows, -1, -2), jnp.swapaxes(lower_factor, -1, -2))

def kernel_tile(row_points, column_points, column_samples, weight):
    distance = (row_points[0][:, :, None] - column_points[0][:, None, :]) ** 2
    for coord_index in range(1, 3):
        distance = distance + (row_points[coord_index][:, :, None] - column_points[coord_index][:, None, :]) ** 2
    kernel = jnp.exp(-SPREAD * distance) * weight[:, None, None]
    return jnp.einsum('lij,ljr->lir', kernel, column_samples, precision=lax.Precision.HIGHEST)

def reference(points, tree_order, samples, near_leaves, near_counts):
    ordered = jnp.take_along_axis(points.reshape(3, DEVICES, PTS_DEV), tree_order[None], axis=2)
    leaf_points = ordered.reshape(3, LEAVES, LEAF)
    leaf_samples = samples.reshape(LEAVES, LEAF, RANK)

    def device_section(device):
        first = device * LEAVES_DEV
        own_points = lax.dynamic_slice_in_dim(leaf_points, first, LEAVES_DEV, 1)
        own_samples = lax.dynamic_slice_in_dim(leaf_samples, first, LEAVES_DEV, 0)
        lists = lax.dynamic_slice_in_dim(near_leaves, first, LEAVES_DEV, 0)
        counts = lax.dynamic_slice_in_dim(near_counts, first, LEAVES_DEV, 0)
        sampled = kernel_tile(own_points, own_points, own_samples, jnp.ones((LEAVES_DEV,), jnp.float32))
        for position in range(MAXNB):
            column_leaf = jnp.clip(first - HALO + lists[:, position], 0, LEAVES - 1).astype(jnp.int32)
            weight = (counts > position).astype(jnp.float32)
            sampled = sampled + kernel_tile(own_points, leaf_points[:, column_leaf], leaf_samples[column_leaf], weight)
        return orthonormalize(sampled)
    leaf_basis, leaf_factor = lax.map(device_section, jnp.arange(DEVICES, dtype=jnp.int32))
    factors = leaf_factor.reshape(LEAVES, RANK, RANK)
    local_levels = []
    while factors.shape[0] > DEVICES:
        basis, factors = orthonormalize(factors.reshape(factors.shape[0] // 2, 2 * RANK, RANK))
        local_levels.append(basis.reshape(DEVICES, -1, 2 * RANK, RANK))
    local_bases = jnp.concatenate(local_levels, axis=1).reshape(DEVICES * (LEAVES_DEV - 1), 2 * RANK, RANK)
    upper_levels = []
    height = 0
    while factors.shape[0] > 1:
        basis, factors = orthonormalize(factors.reshape(factors.shape[0] // 2, 2 * RANK, RANK))
        height = height + 1
        upper_levels.append(jnp.repeat(basis, 2 ** height, axis=0))
    upper_bases = jnp.stack(upper_levels, axis=1).reshape(DEVICES * LEVELS, 2 * RANK, RANK)
    return (leaf_basis.reshape(NPTS, RANK), local_bases, upper_bases, factors[0])
```

```python
import functools

import jax
import jax.numpy as jnp
from jax import lax
from jax.experimental import pallas as pl
from jax.experimental.pallas import tpu as pltpu
from jax.sharding import PartitionSpec as P

HALO = 2
MAXNB = 5
PANEL = 32


SPREAD = 50.0


def passed_along(block, axis, distance):
    devices = range(lax.axis_size(axis))
    route = [(i - distance, i) for i in devices if i - distance in devices]
    return lax.ppermute(block, axis, route)


def from_partner(value, axis, stride):
    mask = 2**stride
    pairs = [(source, source ^ mask) for source in range(lax.axis_size(axis))]
    return lax.ppermute(value, axis, pairs)


def kernel_tile(row_points, column_points, column_samples, weight):
    distance = (row_points[0][:, :, None] - column_points[0][:, None, :]) ** 2
    for coord_index in range(1, 3):
        distance = (
            distance
            + (row_points[coord_index][:, :, None] - column_points[coord_index][:, None, :]) ** 2
        )
    kernel = jnp.exp(-SPREAD * distance) * weight[:, None, None]
    return jnp.einsum("lij,ljr->lir", kernel, column_samples, precision=lax.Precision.HIGHEST)


def dot(a, b, contract_a=1, contract_b=0):
    return lax.dot_general(
        a,
        b,
        (((contract_a,), (contract_b,)), ((), ())),
        precision=lax.Precision.HIGHEST,
        preferred_element_type=jnp.float32,
    )


def eliminate(work, first, count):
    size = work.shape[-1]
    chunks = PANEL // 8
    lane = lax.broadcasted_iota(jnp.int32, (1, 1, size), 2)
    sub = lax.broadcasted_iota(jnp.int32, (1, 8, size), 1)
    group = pl.ds(first, count)
    for top in range(0, size, PANEL):
        parts = [work[group, top + 8 * t : top + 8 * t + 8, :] for t in range(chunks)]
        for k in range(PANEL):
            own, s = k // 8, k % 8
            here = lane == top + k
            columns = {
                t: jnp.broadcast_to(parts[t][:, :, top + k : top + k + 1], parts[t].shape)
                for t in range(own, chunks)
            }
            d = columns[own][:, s : s + 1, :]
            r = lax.rsqrt(d)
            r = r * (1.5 - 0.5 * d * r * r)
            row = jnp.where(here, r, parts[own][:, s : s + 1, :] * r)
            for t in range(own, chunks):
                new = jnp.where(here, 0.0, parts[t]) - (columns[t] * r) * row
                if t == own:
                    new = jnp.where(sub > s, new, jnp.where(sub == s, row, parts[t]))
                parts[t] = new
        for t in range(chunks):
            work[group, top + 8 * t : top + 8 * t + 8, :] = parts[t]
        below = top + PANEL
        if below < size:
            rows_id = lax.broadcasted_iota(jnp.int32, (PANEL, size), 0) + top
            lane2 = lax.broadcasted_iota(jnp.int32, (PANEL, size), 1)
            in_panel = (lane2 >= top) & (lane2 < below)
            for g in range(count):
                panel = work[first + g, top:below, :]
                left = panel.T[below:, :]
                right = jnp.where(in_panel & (lane2 > rows_id), 0.0, panel)
                lane3 = lax.broadcasted_iota(jnp.int32, (size - below, size), 1)
                old = work[first + g, below:, :]
                old = jnp.where((lane3 >= top) & (lane3 < below), 0.0, old)
                work[first + g, below:, :] = old - dot(left, right)


def split_factor(w):
    row = lax.broadcasted_iota(jnp.int32, w.shape, 0)
    column = lax.broadcasted_iota(jnp.int32, w.shape, 1)
    upper = jnp.where(row < column, w, jnp.where(row == column, 1.0 / w, 0.0))
    return upper, jnp.where(row >= column, w, 0.0)


def local_kernel(gram_ref, sampled_ref, leaf_ref, local_ref, work):
    leaves = gram_ref.shape[0]
    nodes = 2 * leaves - 1
    rank = gram_ref.shape[-1]
    work[pl.ds(0, leaves)] = gram_ref[...]
    for node in range(leaves, nodes):
        child = 2 * (node - leaves)
        work[node] = work[child] + work[child + 1]
    eliminate(work, 0, leaves)
    eliminate(work, leaves, leaves - 1)
    for leaf in range(leaves):
        leaf_ref[leaf] = dot(sampled_ref[leaf], split_factor(work[leaf])[1], 1, 1)
    for node in range(leaves, nodes):
        child = 2 * (node - leaves)
        inverse = split_factor(work[node])[1]
        for half in range(2):
            factor = split_factor(work[child + half])[0]
            local_ref[node - leaves, half * rank : (half + 1) * rank, :] = dot(
                factor, inverse, 1, 1
            )


def upper_kernel(position, gram_ref, upper_ref, root_ref, work):
    levels = upper_ref.shape[0]
    rank = gram_ref.shape[-1]
    count = 2 * levels + 1
    work[...] = gram_ref[...]
    eliminate(work, 0, count)
    index = position()
    for level in range(levels):
        inverse = split_factor(work[level + 1])[1]
        own = split_factor(work[level])[0]
        partner = split_factor(work[levels + 1 + level])[0]
        second = index // 2**level % 2 == 1
        upper_ref[level, :rank, :] = dot(jnp.where(second, partner, own), inverse, 1, 1)
        upper_ref[level, rank:, :] = dot(jnp.where(second, own, partner), inverse, 1, 1)
    root_ref[...] = split_factor(work[levels])[0]


def per_device(points, tree_order, samples, near_leaves, near_counts):
    leaves = near_counts.shape[0]
    rank_width = samples.shape[1]
    leaf_size = samples.shape[0] // leaves
    ordered = jnp.take(points, tree_order[0], axis=1)
    edge_rows = HALO * leaf_size
    before_points, before_samples = passed_along(
        (ordered[:, -edge_rows:], samples[-edge_rows:]), ("tx", "ty"), 1
    )
    after_points, after_samples = passed_along(
        (ordered[:, :edge_rows], samples[:edge_rows]), ("tx", "ty"), -1
    )
    window_width = leaves + 2 * HALO
    window_points = jnp.concatenate([before_points, ordered, after_points], axis=1).reshape(
        3, window_width, leaf_size
    )
    window_samples = jnp.concatenate([before_samples, samples, after_samples], axis=0).reshape(
        window_width, leaf_size, rank_width
    )
    own_points = ordered.reshape(3, leaves, leaf_size)
    own_samples = samples.reshape(leaves, leaf_size, rank_width)
    sampled = kernel_tile(own_points, own_points, own_samples, jnp.ones((leaves,), jnp.float32))
    for position in range(MAXNB):
        column_leaf = near_leaves[:, position]
        weight = (near_counts > position).astype(jnp.float32)
        sampled = sampled + kernel_tile(
            own_points,
            jnp.take(window_points, column_leaf, axis=1),
            jnp.take(window_samples, column_leaf, axis=0),
            weight,
        )
    grams = jnp.einsum("lir,lis->lrs", sampled, sampled, precision=lax.Precision.HIGHEST)

    own = grams.reshape(leaves, rank_width, rank_width)
    while own.shape[0] > 1:
        own = own[0::2] + own[1::2]
    own_levels, partner_levels = [own[0]], []
    for axis in ("ty", "tx"):
        for height in range(lax.axis_size(axis).bit_length() - 1):
            partner_levels.append(from_partner(own_levels[-1], axis, height))
            own_levels.append(own_levels[-1] + partner_levels[-1])
    levels = len(partner_levels)

    matrix = (rank_width, rank_width)
    vmem = pl.BlockSpec(memory_space=pltpu.VMEM)
    leaf_basis, local_bases = pl.pallas_call(
        local_kernel,
        out_shape=(
            jax.ShapeDtypeStruct((leaves, leaf_size, rank_width), jnp.float32),
            jax.ShapeDtypeStruct((leaves - 1, 2 * rank_width, rank_width), jnp.float32),
        ),
        in_specs=[vmem, vmem],
        out_specs=(vmem, vmem),
        scratch_shapes=[pltpu.VMEM((2 * leaves - 1, *matrix), jnp.float32)],
        compiler_params=pltpu.CompilerParams(vmem_limit_bytes=32 * 2**20),
        name="local_nodes",
    )(grams, sampled)

    def position():
        return lax.axis_index("tx") * lax.axis_size("ty") + lax.axis_index("ty")

    upper_bases, root = pl.pallas_call(
        functools.partial(upper_kernel, position),
        out_shape=(
            jax.ShapeDtypeStruct((levels, 2 * rank_width, rank_width), jnp.float32),
            jax.ShapeDtypeStruct(matrix, jnp.float32),
        ),
        in_specs=[vmem],
        out_specs=(vmem, vmem),
        scratch_shapes=[pltpu.VMEM((2 * levels + 1, *matrix), jnp.float32)],
        compiler_params=pltpu.CompilerParams(vmem_limit_bytes=32 * 2**20),
        name="upper_nodes",
    )(jnp.stack(own_levels + partner_levels))
    return (leaf_basis.reshape(leaves * leaf_size, rank_width), local_bases, upper_bases, root)


def solution(mesh):
    return jax.shard_map(
        per_device,
        mesh=mesh,
        in_specs=(
            P(None, ("tx", "ty")),
            P(("tx", "ty"), None),
            P(("tx", "ty"), None),
            P(("tx", "ty"), None),
            P(("tx", "ty")),
        ),
        out_specs=(
            P(("tx", "ty"), None),
            P(("tx", "ty"), None, None),
            P(("tx", "ty"), None, None),
            P(),
        ),
        check_vma=False,
    )
```

```python
import functools

import jax
import jax.numpy as jnp
from jax import lax
from jax.experimental import pallas as pl
from jax.experimental.pallas import tpu as pltpu
from jax.sharding import PartitionSpec as P

HALO = 2
MAXNB = 5
PANEL = 32


SPREAD = 50.0


def from_partner(value, axis, stride):
    mask = 2**stride
    pairs = [(source, source ^ mask) for source in range(lax.axis_size(axis))]
    return lax.ppermute(value, axis, pairs)


def dot(a, b, contract_a=1, contract_b=0):
    return lax.dot_general(
        a,
        b,
        (((contract_a,), (contract_b,)), ((), ())),
        precision=lax.Precision.HIGHEST,
        preferred_element_type=jnp.float32,
    )


def linear_position():
    return lax.axis_index("tx") * lax.axis_size("ty") + lax.axis_index("ty")


def device_at(position):
    across = lax.axis_size("ty")
    return (position // across, position % across)


def sample_kernel(
    near_ref, count_ref, points_ref, order_ref, samples_ref, sampled_ref, gram_ref,
    ordered, before_points, after_points, before_samples, after_samples,
    rows, columns, pieces, tile, send_sems, recv_sems,
):
    me = linear_position()
    devices = lax.axis_size("tx") * lax.axis_size("ty")
    has_before, has_after = me > 0, me < devices - 1
    leaves, leaf_size, rank = sampled_ref.shape
    lines = leaf_size // 128
    edge = HALO * leaf_size

    barrier = pltpu.get_barrier_semaphore()

    @pl.when(has_before)
    def _():
        pl.semaphore_signal(
            barrier, inc=1, device_id=device_at(me - 1), device_id_type=pl.DeviceIdType.MESH
        )

    @pl.when(has_after)
    def _():
        pl.semaphore_signal(
            barrier, inc=1, device_id=device_at(me + 1), device_id_type=pl.DeviceIdType.MESH
        )

    order = order_ref[...]
    place, line = order % 128, order // 128
    for coord in range(3):
        picked = jnp.zeros(order.shape, jnp.float32)
        for a in range(order.shape[0]):
            source = jnp.broadcast_to(points_ref[coord, a : a + 1, :], order.shape)
            gathered = jnp.take_along_axis(source, place, axis=1, mode="promise_in_bounds")
            picked = jnp.where(line == a, gathered, picked)
        ordered[coord] = picked

    pl.semaphore_wait(barrier, has_before.astype(jnp.int32) + has_after.astype(jnp.int32))

    def copy(index, source, target, position):
        return pltpu.make_async_remote_copy(
            src_ref=source,
            dst_ref=target,
            send_sem=send_sems.at[index],
            recv_sem=recv_sems.at[index],
            device_id=device_at(position),
            device_id_type=pl.DeviceIdType.MESH,
        )

    own_rows = samples_ref.shape[0]
    to_after = [
        copy(0, samples_ref.at[pl.ds(own_rows - edge, edge)], before_samples, me + 1),
        copy(1, ordered, before_points, me + 1),
    ]
    to_before = [
        copy(2, samples_ref.at[pl.ds(0, edge)], after_samples, me - 1),
        copy(3, ordered, after_points, me - 1),
    ]

    @pl.when(has_after)
    def _():
        for c in to_after:
            c.start()

    @pl.when(has_before)
    def _():
        for c in to_before:
            c.start()

    def place_leaf(window_leaf, points, leaf, samples):
        for coord in range(3):
            rows[window_leaf, coord : coord + 1, :] = jnp.concatenate(
                [points[coord, leaf * lines + n : leaf * lines + n + 1, :] for n in range(lines)],
                axis=1,
            )
        high = samples.astype(jnp.bfloat16)
        low = (samples - high.astype(jnp.float32)).astype(jnp.bfloat16)
        pieces[window_leaf] = jnp.concatenate([high, low], axis=1)

    for leaf in range(leaves):
        place_leaf(
            HALO + leaf, ordered, leaf, samples_ref[leaf * leaf_size : (leaf + 1) * leaf_size, :]
        )
        for coord in range(3):
            for n in range(lines):
                wide = jnp.broadcast_to(
                    ordered[coord, leaf * lines + n : leaf * lines + n + 1, :], (128, 128)
                )
                columns[coord, leaf, n * 128 : (n + 1) * 128, :] = wide.T

    def tile_product(leaf, window_leaf, weight):
        others = rows[window_leaf]
        chunk = 64
        for start in range(0, leaf_size, chunk):
            distance = 0.0
            for coord in range(3):
                own = columns[coord, leaf, start : start + chunk, :]
                own = jnp.concatenate([own] * lines, axis=1)
                gap = own - others[coord : coord + 1, :]
                distance = distance + gap * gap
            value = jnp.exp(-SPREAD * distance)
            if weight is not None:
                value = value * weight
            high = value.astype(jnp.bfloat16)
            low = (value - high.astype(jnp.float32)).astype(jnp.bfloat16)
            tile[start : start + chunk, :] = high
            tile[leaf_size + start : leaf_size + start + chunk, :] = low
        product = lax.dot_general(
            tile[...],
            pieces[window_leaf],
            (((1,), (0,)), ((), ())),
            preferred_element_type=jnp.float32,
        )
        product = product[:leaf_size] + product[leaf_size:]
        return product[:, :rank] + product[:, rank:]

    @pl.loop(0, leaves)
    def _(leaf):
        sampled_ref[leaf] = tile_product(leaf, HALO + leaf, None)

    @pl.when(has_before)
    def _():
        copy(0, samples_ref.at[pl.ds(0, edge)], before_samples, me - 1).wait_recv()
        copy(1, ordered, before_points, me - 1).wait_recv()

    @pl.when(has_after)
    def _():
        copy(2, samples_ref.at[pl.ds(0, edge)], after_samples, me + 1).wait_recv()
        copy(3, ordered, after_points, me + 1).wait_recv()

    @pl.when(jnp.logical_not(has_before))
    def _():
        before_samples[...] = jnp.zeros_like(before_samples)
        before_points[...] = jnp.zeros_like(before_points)

    @pl.when(jnp.logical_not(has_after))
    def _():
        after_samples[...] = jnp.zeros_like(after_samples)
        after_points[...] = jnp.zeros_like(after_points)

    for h in range(HALO):
        part = slice(h * leaf_size, (h + 1) * leaf_size)
        place_leaf(h, before_points, leaves - HALO + h, before_samples[part, :])
        place_leaf(HALO + leaves + h, after_points, h, after_samples[part, :])

    @pl.loop(0, leaves)
    def _(leaf):
        total = sampled_ref[leaf]
        for k in range(MAXNB):
            weight = (count_ref[leaf] > k).astype(jnp.float32)
            total = total + tile_product(leaf, near_ref[leaf, k], weight)
        sampled_ref[leaf] = total
        gram_ref[leaf] = dot(total, total, 0, 0)

    @pl.when(has_after)
    def _():
        for c in to_after:
            c.wait_send()

    @pl.when(has_before)
    def _():
        for c in to_before:
            c.wait_send()


def sample_leaves(points, tree_order, samples, near_leaves, near_counts):
    leaves = near_counts.shape[0]
    rank = samples.shape[1]
    leaf_size = samples.shape[0] // leaves
    lines = points.shape[1] // 128
    window = leaves + 2 * HALO
    edge = HALO * leaf_size
    vmem = pl.BlockSpec(memory_space=pltpu.VMEM)
    smem = pl.BlockSpec(memory_space=pltpu.SMEM)
    block = (3, lines, 128)
    return pl.pallas_call(
        sample_kernel,
        out_shape=(
            jax.ShapeDtypeStruct((leaves, leaf_size, rank), jnp.float32),
            jax.ShapeDtypeStruct((leaves, rank, rank), jnp.float32),
        ),
        in_specs=[smem, smem, vmem, vmem, vmem],
        out_specs=(vmem, vmem),
        scratch_shapes=[
            pltpu.VMEM(block, jnp.float32),
            pltpu.VMEM(block, jnp.float32),
            pltpu.VMEM(block, jnp.float32),
            pltpu.VMEM((edge, rank), jnp.float32),
            pltpu.VMEM((edge, rank), jnp.float32),
            pltpu.VMEM((window, 8, leaf_size), jnp.float32),
            pltpu.VMEM((3, leaves, leaf_size, 128), jnp.float32),
            pltpu.VMEM((window, leaf_size, 2 * rank), jnp.bfloat16),
            pltpu.VMEM((2 * leaf_size, leaf_size), jnp.bfloat16),
            pltpu.SemaphoreType.DMA((4,)),
            pltpu.SemaphoreType.DMA((4,)),
        ],
        compiler_params=pltpu.CompilerParams(
            vmem_limit_bytes=40 * 2**20, collective_id=0, has_side_effects=True
        ),
        name="sample_leaves",
    )(
        near_leaves,
        near_counts,
        points.reshape(block),
        tree_order.reshape(lines, 128),
        samples,
    )


def eliminate(work, first, count):
    size = work.shape[-1]
    chunks = PANEL // 8
    lane = lax.broadcasted_iota(jnp.int32, (1, 1, size), 2)
    sub = lax.broadcasted_iota(jnp.int32, (1, 8, size), 1)
    group = pl.ds(first, count)
    for top in range(0, size, PANEL):
        parts = [work[group, top + 8 * t : top + 8 * t + 8, :] for t in range(chunks)]
        for k in range(PANEL):
            own, s = k // 8, k % 8
            here = lane == top + k
            columns = {
                t: jnp.broadcast_to(parts[t][:, :, top + k : top + k + 1], parts[t].shape)
                for t in range(own, chunks)
            }
            d = columns[own][:, s : s + 1, :]
            r = lax.rsqrt(d)
            r = r * (1.5 - 0.5 * d * r * r)
            row = jnp.where(here, r, parts[own][:, s : s + 1, :] * r)
            for t in range(own, chunks):
                new = jnp.where(here, 0.0, parts[t]) - (columns[t] * r) * row
                if t == own:
                    new = jnp.where(sub > s, new, jnp.where(sub == s, row, parts[t]))
                parts[t] = new
        for t in range(chunks):
            work[group, top + 8 * t : top + 8 * t + 8, :] = parts[t]
        below = top + PANEL
        if below < size:
            rows_id = lax.broadcasted_iota(jnp.int32, (PANEL, size), 0) + top
            lane2 = lax.broadcasted_iota(jnp.int32, (PANEL, size), 1)
            in_panel = (lane2 >= top) & (lane2 < below)
            for g in range(count):
                panel = work[first + g, top:below, :]
                left = panel.T[below:, :]
                right = jnp.where(in_panel & (lane2 > rows_id), 0.0, panel)
                lane3 = lax.broadcasted_iota(jnp.int32, (size - below, size), 1)
                old = work[first + g, below:, :]
                old = jnp.where((lane3 >= top) & (lane3 < below), 0.0, old)
                work[first + g, below:, :] = old - dot(left, right)


def split_factor(w):
    row = lax.broadcasted_iota(jnp.int32, w.shape, 0)
    column = lax.broadcasted_iota(jnp.int32, w.shape, 1)
    upper = jnp.where(row < column, w, jnp.where(row == column, 1.0 / w, 0.0))
    return upper, jnp.where(row >= column, w, 0.0)


def local_kernel(gram_ref, sampled_ref, leaf_ref, local_ref, work):
    leaves = gram_ref.shape[0]
    nodes = 2 * leaves - 1
    rank = gram_ref.shape[-1]
    work[pl.ds(0, leaves)] = gram_ref[...]
    for node in range(leaves, nodes):
        child = 2 * (node - leaves)
        work[node] = work[child] + work[child + 1]
    eliminate(work, 0, leaves)
    eliminate(work, leaves, leaves - 1)
    for leaf in range(leaves):
        leaf_ref[leaf] = dot(sampled_ref[leaf], split_factor(work[leaf])[1], 1, 1)
    for node in range(leaves, nodes):
        child = 2 * (node - leaves)
        inverse = split_factor(work[node])[1]
        for half in range(2):
            factor = split_factor(work[child + half])[0]
            local_ref[node - leaves, half * rank : (half + 1) * rank, :] = dot(
                factor, inverse, 1, 1
            )


def upper_kernel(position, gram_ref, upper_ref, root_ref, work):
    levels = upper_ref.shape[0]
    rank = gram_ref.shape[-1]
    count = 2 * levels + 1
    work[...] = gram_ref[...]
    eliminate(work, 0, count)
    index = position()
    for level in range(levels):
        inverse = split_factor(work[level + 1])[1]
        own = split_factor(work[level])[0]
        partner = split_factor(work[levels + 1 + level])[0]
        second = index // 2**level % 2 == 1
        upper_ref[level, :rank, :] = dot(jnp.where(second, partner, own), inverse, 1, 1)
        upper_ref[level, rank:, :] = dot(jnp.where(second, own, partner), inverse, 1, 1)
    root_ref[...] = split_factor(work[levels])[0]


def per_device(points, tree_order, samples, near_leaves, near_counts):
    leaves = near_counts.shape[0]
    rank_width = samples.shape[1]
    leaf_size = samples.shape[0] // leaves
    sampled, grams = sample_leaves(points, tree_order, samples, near_leaves, near_counts)

    own = grams.reshape(leaves, rank_width, rank_width)
    while own.shape[0] > 1:
        own = own[0::2] + own[1::2]
    own_levels, partner_levels = [own[0]], []
    for axis in ("ty", "tx"):
        for height in range(lax.axis_size(axis).bit_length() - 1):
            partner_levels.append(from_partner(own_levels[-1], axis, height))
            own_levels.append(own_levels[-1] + partner_levels[-1])
    levels = len(partner_levels)

    matrix = (rank_width, rank_width)
    vmem = pl.BlockSpec(memory_space=pltpu.VMEM)
    leaf_basis, local_bases = pl.pallas_call(
        local_kernel,
        out_shape=(
            jax.ShapeDtypeStruct((leaves, leaf_size, rank_width), jnp.float32),
            jax.ShapeDtypeStruct((leaves - 1, 2 * rank_width, rank_width), jnp.float32),
        ),
        in_specs=[vmem, vmem],
        out_specs=(vmem, vmem),
        scratch_shapes=[pltpu.VMEM((2 * leaves - 1, *matrix), jnp.float32)],
        compiler_params=pltpu.CompilerParams(vmem_limit_bytes=32 * 2**20),
        name="local_nodes",
    )(grams, sampled)

    def position():
        return lax.axis_index("tx") * lax.axis_size("ty") + lax.axis_index("ty")

    upper_bases, root = pl.pallas_call(
        functools.partial(upper_kernel, position),
        out_shape=(
            jax.ShapeDtypeStruct((levels, 2 * rank_width, rank_width), jnp.float32),
            jax.ShapeDtypeStruct(matrix, jnp.float32),
        ),
        in_specs=[vmem],
        out_specs=(vmem, vmem),
        scratch_shapes=[pltpu.VMEM((2 * levels + 1, *matrix), jnp.float32)],
        compiler_params=pltpu.CompilerParams(vmem_limit_bytes=32 * 2**20),
        name="upper_nodes",
    )(jnp.stack(own_levels + partner_levels))
    return (leaf_basis.reshape(leaves * leaf_size, rank_width), local_bases, upper_bases, root)


def solution(mesh):
    return jax.shard_map(
        per_device,
        mesh=mesh,
        in_specs=(
            P(None, ("tx", "ty")),
            P(("tx", "ty"), None),
            P(("tx", "ty"), None),
            P(("tx", "ty"), None),
            P(("tx", "ty")),
        ),
        out_specs=(
            P(("tx", "ty"), None),
            P(("tx", "ty"), None, None),
            P(("tx", "ty"), None, None),
            P(),
        ),
        check_vma=False,
    )
```

```python
import functools

import jax
import jax.numpy as jnp
from jax import lax
from jax.experimental import pallas as pl
from jax.experimental.pallas import tpu as pltpu
from jax.sharding import PartitionSpec as P

HALO = 2
MAXNB = 5
PANEL = 32


SPREAD = 50.0


def dot(a, b, contract_a=1, contract_b=0):
    return lax.dot_general(
        a,
        b,
        (((contract_a,), (contract_b,)), ((), ())),
        precision=lax.Precision.HIGHEST,
        preferred_element_type=jnp.float32,
    )


def linear_position():
    return lax.axis_index("tx") * lax.axis_size("ty") + lax.axis_index("ty")


def device_at(position):
    across = lax.axis_size("ty")
    return (position // across, position % across)


def sample_kernel(
    near_ref, count_ref, points_ref, order_ref, samples_ref, sampled_ref, gram_ref,
    ordered, before_points, after_points, before_samples, after_samples,
    rows, columns, pieces, tile, send_sems, recv_sems,
):
    me = linear_position()
    devices = lax.axis_size("tx") * lax.axis_size("ty")
    has_before, has_after = me > 0, me < devices - 1
    leaves, leaf_size, rank = sampled_ref.shape
    lines = leaf_size // 128
    edge = HALO * leaf_size

    barrier = pltpu.get_barrier_semaphore()

    @pl.when(has_before)
    def _():
        pl.semaphore_signal(
            barrier, inc=1, device_id=device_at(me - 1), device_id_type=pl.DeviceIdType.MESH
        )

    @pl.when(has_after)
    def _():
        pl.semaphore_signal(
            barrier, inc=1, device_id=device_at(me + 1), device_id_type=pl.DeviceIdType.MESH
        )

    order = order_ref[...]
    place, line = order % 128, order // 128
    for coord in range(3):
        picked = jnp.zeros(order.shape, jnp.float32)
        for a in range(order.shape[0]):
            source = jnp.broadcast_to(points_ref[coord, a : a + 1, :], order.shape)
            gathered = jnp.take_along_axis(source, place, axis=1, mode="promise_in_bounds")
            picked = jnp.where(line == a, gathered, picked)
        ordered[coord] = picked

    pl.semaphore_wait(barrier, has_before.astype(jnp.int32) + has_after.astype(jnp.int32))

    def copy(index, source, target, position):
        return pltpu.make_async_remote_copy(
            src_ref=source,
            dst_ref=target,
            send_sem=send_sems.at[index],
            recv_sem=recv_sems.at[index],
            device_id=device_at(position),
            device_id_type=pl.DeviceIdType.MESH,
        )

    own_rows = samples_ref.shape[0]
    to_after = [
        copy(0, samples_ref.at[pl.ds(own_rows - edge, edge)], before_samples, me + 1),
        copy(1, ordered, before_points, me + 1),
    ]
    to_before = [
        copy(2, samples_ref.at[pl.ds(0, edge)], after_samples, me - 1),
        copy(3, ordered, after_points, me - 1),
    ]

    @pl.when(has_after)
    def _():
        for c in to_after:
            c.start()

    @pl.when(has_before)
    def _():
        for c in to_before:
            c.start()

    def place_leaf(window_leaf, points, leaf, samples):
        for coord in range(3):
            rows[window_leaf, coord : coord + 1, :] = jnp.concatenate(
                [points[coord, leaf * lines + n : leaf * lines + n + 1, :] for n in range(lines)],
                axis=1,
            )
        high = samples.astype(jnp.bfloat16)
        low = (samples - high.astype(jnp.float32)).astype(jnp.bfloat16)
        pieces[window_leaf] = jnp.concatenate([high, low], axis=1)

    for leaf in range(leaves):
        place_leaf(
            HALO + leaf, ordered, leaf, samples_ref[leaf * leaf_size : (leaf + 1) * leaf_size, :]
        )
        for coord in range(3):
            for n in range(lines):
                wide = jnp.broadcast_to(
                    ordered[coord, leaf * lines + n : leaf * lines + n + 1, :], (128, 128)
                )
                columns[coord, leaf, n * 128 : (n + 1) * 128, :] = wide.T

    def tile_product(leaf, window_leaf, weight):
        others = rows[window_leaf]
        chunk = 64
        for start in range(0, leaf_size, chunk):
            distance = 0.0
            for coord in range(3):
                own = columns[coord, leaf, start : start + chunk, :]
                own = jnp.concatenate([own] * lines, axis=1)
                gap = own - others[coord : coord + 1, :]
                distance = distance + gap * gap
            value = jnp.exp(-SPREAD * distance)
            if weight is not None:
                value = value * weight
            high = value.astype(jnp.bfloat16)
            low = (value - high.astype(jnp.float32)).astype(jnp.bfloat16)
            tile[start : start + chunk, :] = high
            tile[leaf_size + start : leaf_size + start + chunk, :] = low
        product = lax.dot_general(
            tile[...],
            pieces[window_leaf],
            (((1,), (0,)), ((), ())),
            preferred_element_type=jnp.float32,
        )
        product = product[:leaf_size] + product[leaf_size:]
        return product[:, :rank] + product[:, rank:]

    @pl.loop(0, leaves)
    def _(leaf):
        sampled_ref[leaf] = tile_product(leaf, HALO + leaf, None)

    @pl.when(has_before)
    def _():
        copy(0, samples_ref.at[pl.ds(0, edge)], before_samples, me - 1).wait_recv()
        copy(1, ordered, before_points, me - 1).wait_recv()

    @pl.when(has_after)
    def _():
        copy(2, samples_ref.at[pl.ds(0, edge)], after_samples, me + 1).wait_recv()
        copy(3, ordered, after_points, me + 1).wait_recv()

    @pl.when(jnp.logical_not(has_before))
    def _():
        before_samples[...] = jnp.zeros_like(before_samples)
        before_points[...] = jnp.zeros_like(before_points)

    @pl.when(jnp.logical_not(has_after))
    def _():
        after_samples[...] = jnp.zeros_like(after_samples)
        after_points[...] = jnp.zeros_like(after_points)

    for h in range(HALO):
        part = slice(h * leaf_size, (h + 1) * leaf_size)
        place_leaf(h, before_points, leaves - HALO + h, before_samples[part, :])
        place_leaf(HALO + leaves + h, after_points, h, after_samples[part, :])

    @pl.loop(0, leaves)
    def _(leaf):
        total = sampled_ref[leaf]
        for k in range(MAXNB):
            weight = (count_ref[leaf] > k).astype(jnp.float32)
            total = total + tile_product(leaf, near_ref[leaf, k], weight)
        sampled_ref[leaf] = total
        gram_ref[leaf] = dot(total, total, 0, 0)

    @pl.when(has_after)
    def _():
        for c in to_after:
            c.wait_send()

    @pl.when(has_before)
    def _():
        for c in to_before:
            c.wait_send()


def sample_leaves(points, tree_order, samples, near_leaves, near_counts):
    leaves = near_counts.shape[0]
    rank = samples.shape[1]
    leaf_size = samples.shape[0] // leaves
    lines = points.shape[1] // 128
    window = leaves + 2 * HALO
    edge = HALO * leaf_size
    vmem = pl.BlockSpec(memory_space=pltpu.VMEM)
    smem = pl.BlockSpec(memory_space=pltpu.SMEM)
    block = (3, lines, 128)
    return pl.pallas_call(
        sample_kernel,
        out_shape=(
            jax.ShapeDtypeStruct((leaves, leaf_size, rank), jnp.float32),
            jax.ShapeDtypeStruct((leaves, rank, rank), jnp.float32),
        ),
        in_specs=[smem, smem, vmem, vmem, vmem],
        out_specs=(vmem, vmem),
        scratch_shapes=[
            pltpu.VMEM(block, jnp.float32),
            pltpu.VMEM(block, jnp.float32),
            pltpu.VMEM(block, jnp.float32),
            pltpu.VMEM((edge, rank), jnp.float32),
            pltpu.VMEM((edge, rank), jnp.float32),
            pltpu.VMEM((window, 8, leaf_size), jnp.float32),
            pltpu.VMEM((3, leaves, leaf_size, 128), jnp.float32),
            pltpu.VMEM((window, leaf_size, 2 * rank), jnp.bfloat16),
            pltpu.VMEM((2 * leaf_size, leaf_size), jnp.bfloat16),
            pltpu.SemaphoreType.DMA((4,)),
            pltpu.SemaphoreType.DMA((4,)),
        ],
        compiler_params=pltpu.CompilerParams(
            vmem_limit_bytes=40 * 2**20, collective_id=0, has_side_effects=True
        ),
        name="sample_leaves",
    )(
        near_leaves,
        near_counts,
        points.reshape(block),
        tree_order.reshape(lines, 128),
        samples,
    )


def three_terms(x):
    high = x.astype(jnp.bfloat16)
    rest = x - high.astype(jnp.float32)
    middle = rest.astype(jnp.bfloat16)
    low = (rest - middle.astype(jnp.float32)).astype(jnp.bfloat16)
    return high, middle, low


def gram_product(left, right):
    a, b, c = three_terms(left)
    d, e, f = three_terms(right)
    return lax.dot_general(
        jnp.concatenate([a, a, b, a, b, c], axis=0),
        jnp.concatenate([d, e, d, f, e, d], axis=0),
        (((0,), (0,)), ((), ())),
        preferred_element_type=jnp.float32,
    )


def eliminate(work, first, count):
    size = work.shape[-1]
    chunks = PANEL // 8
    lane = lax.broadcasted_iota(jnp.int32, (1, 8, size), 2)
    sub = lax.broadcasted_iota(jnp.int32, (1, 8, size), 1)
    group = pl.ds(first, count)
    for top in range(0, size, PANEL):
        parts = [work[group, top + 8 * t : top + 8 * t + 8, :] for t in range(chunks)]
        for own in range(chunks):
            pivots = jnp.ones_like(parts[own])
            for s in range(8):
                k = top + 8 * own + s
                here = lane == k
                columns = [
                    jnp.broadcast_to(parts[t][:, :, k : k + 1], parts[t].shape)
                    for t in range(own, chunks)
                ]
                d = columns[0][:, s : s + 1, :]
                inverse = pl.reciprocal(d, approx=True)
                inverse = inverse * (2.0 - d * inverse)
                pivots = jnp.where(sub == s, d, pivots)
                row = jnp.where(here[:, :1], 1.0, parts[own][:, s : s + 1, :])
                for t in range(own, chunks):
                    step = (columns[t - own] * row) * inverse
                    if t == own:
                        step = jnp.where(sub > s, step, 0.0)
                        kept = jnp.where(sub == s, 1.0, 0.0)
                        parts[t] = jnp.where(here & (sub >= s), kept, parts[t]) - step
                    else:
                        parts[t] = jnp.where(here, 0.0, parts[t]) - step
            scale = lax.rsqrt(pivots)
            scale = scale * (1.5 - 0.5 * pivots * scale * scale)
            work[group, top + 8 * own : top + 8 * own + 8, :] = parts[own] * scale
        below = top + PANEL
        if below < size:
            rows_id = lax.broadcasted_iota(jnp.int32, (PANEL, size), 0) + top
            lane2 = lax.broadcasted_iota(jnp.int32, (PANEL, size), 1)
            in_panel = (lane2 >= top) & (lane2 < below)
            lane3 = lax.broadcasted_iota(jnp.int32, (size - below, size), 1)
            cleared = (lane3 >= top) & (lane3 < below)
            for g in range(count):
                panel = work[first + g, top:below, :]
                right = jnp.where(in_panel & (lane2 > rows_id), 0.0, panel)
                old = jnp.where(cleared, 0.0, work[first + g, below:, :])
                work[first + g, below:, :] = old - gram_product(panel, right)[below:]


def split_factor(w):
    row = lax.broadcasted_iota(jnp.int32, w.shape, 0)
    column = lax.broadcasted_iota(jnp.int32, w.shape, 1)
    upper = jnp.where(row < column, w, jnp.where(row == column, 1.0 / w, 0.0))
    return upper, jnp.where(row >= column, w, 0.0)


def node_kernel(
    gram_ref, sampled_ref, leaf_ref, local_ref, upper_ref, root_ref,
    work, sums, partner_sums, factors, partner_factors,
    sum_send, sum_recv, factor_send, factor_recv,
):
    leaves = gram_ref.shape[0]
    nodes = 2 * leaves - 1
    rank = gram_ref.shape[-1]
    levels = upper_ref.shape[0]
    me = linear_position()

    def partner(level):
        return device_at(me + (1 - me // 2**level % 2 * 2) * 2**level)

    barrier = pltpu.get_barrier_semaphore()
    for level in range(levels):
        pl.semaphore_signal(
            barrier, inc=1, device_id=partner(level), device_id_type=pl.DeviceIdType.MESH
        )

    work[pl.ds(0, leaves)] = gram_ref[...]
    for node in range(leaves, nodes):
        child = 2 * (node - leaves)
        work[node] = work[child] + work[child + 1]
    sums[0] = work[nodes - 1]
    pl.semaphore_wait(barrier, levels)

    def copy(level, source, target, send, recv):
        return pltpu.make_async_remote_copy(
            src_ref=source.at[level],
            dst_ref=target.at[level],
            send_sem=send.at[level],
            recv_sem=recv.at[level],
            device_id=partner(level),
            device_id_type=pl.DeviceIdType.MESH,
        )

    sum_copies = [copy(h, sums, partner_sums, sum_send, sum_recv) for h in range(levels)]
    factor_copies = [
        copy(h, factors, partner_factors, factor_send, factor_recv) for h in range(levels)
    ]

    def climb(level):
        if level < levels:
            sum_copies[level].wait_recv()
            sums[level + 1] = sums[level] + partner_sums[level]
            if level + 1 < levels:
                sum_copies[level + 1].start()

    def leaf_basis(leaf):
        leaf_ref[leaf] = dot(sampled_ref[leaf], split_factor(work[leaf])[1], 1, 1)

    sum_copies[0].start()
    group = max(g for g in range(1, 6) if nodes % g == 0)
    groups = nodes // group

    @pl.loop(0, groups)
    def _(g):
        eliminate(work, g * group, group)
        for level in range(min(groups, levels)):
            pl.when(g == level)(functools.partial(climb, level))

    for leaf in range(leaves // 2):
        leaf_basis(leaf)
    climb(groups)
    for leaf in range(leaves // 2, leaves):
        leaf_basis(leaf)
    for level in range(groups + 1, levels):
        climb(level)
    factors[0] = work[nodes - 1]
    for level in range(1, levels + 1):
        factors[level] = sums[level]
    eliminate(factors, 1, levels)
    for c in factor_copies:
        c.start()
    root_ref[...] = split_factor(factors[levels])[0]
    for node in range(leaves, nodes):
        child = 2 * (node - leaves)
        inverse = split_factor(work[node])[1]
        for half in range(2):
            factor = split_factor(work[child + half])[0]
            local_ref[node - leaves, half * rank : (half + 1) * rank, :] = dot(
                factor, inverse, 1, 1
            )
    for level in range(levels):
        factor_copies[level].wait_recv()
        inverse = split_factor(factors[level + 1])[1]
        own = split_factor(factors[level])[0]
        other = split_factor(partner_factors[level])[0]
        second = me // 2**level % 2 == 1
        upper_ref[level, :rank, :] = dot(jnp.where(second, other, own), inverse, 1, 1)
        upper_ref[level, rank:, :] = dot(jnp.where(second, own, other), inverse, 1, 1)
    for c in sum_copies + factor_copies:
        c.wait_send()


def per_device(points, tree_order, samples, near_leaves, near_counts):
    leaves = near_counts.shape[0]
    rank_width = samples.shape[1]
    leaf_size = samples.shape[0] // leaves
    sampled, grams = sample_leaves(points, tree_order, samples, near_leaves, near_counts)

    devices = lax.axis_size("tx") * lax.axis_size("ty")
    levels = devices.bit_length() - 1
    matrix = (rank_width, rank_width)
    vmem = pl.BlockSpec(memory_space=pltpu.VMEM)
    leaf_basis, local_bases, upper_bases, root = pl.pallas_call(
        node_kernel,
        out_shape=(
            jax.ShapeDtypeStruct((leaves, leaf_size, rank_width), jnp.float32),
            jax.ShapeDtypeStruct((leaves - 1, 2 * rank_width, rank_width), jnp.float32),
            jax.ShapeDtypeStruct((levels, 2 * rank_width, rank_width), jnp.float32),
            jax.ShapeDtypeStruct(matrix, jnp.float32),
        ),
        in_specs=[vmem, vmem],
        out_specs=(vmem,) * 4,
        scratch_shapes=[
            pltpu.VMEM((2 * leaves - 1, *matrix), jnp.float32),
            pltpu.VMEM((levels + 1, *matrix), jnp.float32),
            pltpu.VMEM((levels, *matrix), jnp.float32),
            pltpu.VMEM((levels + 1, *matrix), jnp.float32),
            pltpu.VMEM((levels, *matrix), jnp.float32),
        ]
        + [pltpu.SemaphoreType.DMA((levels,))] * 4,
        compiler_params=pltpu.CompilerParams(
            vmem_limit_bytes=40 * 2**20, collective_id=1, has_side_effects=True
        ),
        name="tree_nodes",
    )(grams, sampled)
    return (leaf_basis.reshape(leaves * leaf_size, rank_width), local_bases, upper_bases, root)


def solution(mesh):
    return jax.shard_map(
        per_device,
        mesh=mesh,
        in_specs=(
            P(None, ("tx", "ty")),
            P(("tx", "ty"), None),
            P(("tx", "ty"), None),
            P(("tx", "ty"), None),
            P(("tx", "ty")),
        ),
        out_specs=(
            P(("tx", "ty"), None),
            P(("tx", "ty"), None, None),
            P(("tx", "ty"), None, None),
            P(),
        ),
        check_vma=False,
    )
```

```python
import functools

import jax
import jax.numpy as jnp
from jax import lax
from jax.experimental import pallas as pl
from jax.experimental.pallas import tpu as pltpu
from jax.sharding import PartitionSpec as P

HALO = 2
MAXNB = 5
PANEL = 32


SPREAD = 50.0


def dot(a, b, contract_a=1, contract_b=0):
    return lax.dot_general(
        a,
        b,
        (((contract_a,), (contract_b,)), ((), ())),
        precision=lax.Precision.HIGHEST,
        preferred_element_type=jnp.float32,
    )


def linear_position():
    return lax.axis_index("tx") * lax.axis_size("ty") + lax.axis_index("ty")


def device_at(position):
    across = lax.axis_size("ty")
    return (position // across, position % across)


def sample_kernel(
    near_ref, count_ref, points_ref, order_ref, samples_ref, sampled_ref, gram_ref,
    ordered, before_points, after_points, before_samples, after_samples,
    rows, columns, pieces, tile, send_sems, recv_sems,
):
    me = linear_position()
    devices = lax.axis_size("tx") * lax.axis_size("ty")
    has_before, has_after = me > 0, me < devices - 1
    leaves, leaf_size, rank = sampled_ref.shape
    lines = leaf_size // 128
    edge = HALO * leaf_size

    barrier = pltpu.get_barrier_semaphore()

    @pl.when(has_before)
    def _():
        pl.semaphore_signal(
            barrier, inc=1, device_id=device_at(me - 1), device_id_type=pl.DeviceIdType.MESH
        )

    @pl.when(has_after)
    def _():
        pl.semaphore_signal(
            barrier, inc=1, device_id=device_at(me + 1), device_id_type=pl.DeviceIdType.MESH
        )

    order = order_ref[...]
    place, line = order % 128, order // 128
    for coord in range(3):
        picked = jnp.zeros(order.shape, jnp.float32)
        for a in range(order.shape[0]):
            source = jnp.broadcast_to(points_ref[coord, a : a + 1, :], order.shape)
            gathered = jnp.take_along_axis(source, place, axis=1, mode="promise_in_bounds")
            picked = jnp.where(line == a, gathered, picked)
        ordered[coord] = picked

    pl.semaphore_wait(barrier, has_before.astype(jnp.int32) + has_after.astype(jnp.int32))

    def copy(index, source, target, position):
        return pltpu.make_async_remote_copy(
            src_ref=source,
            dst_ref=target,
            send_sem=send_sems.at[index],
            recv_sem=recv_sems.at[index],
            device_id=device_at(position),
            device_id_type=pl.DeviceIdType.MESH,
        )

    own_rows = samples_ref.shape[0]
    to_after = [
        copy(0, samples_ref.at[pl.ds(own_rows - edge, edge)], before_samples, me + 1),
        copy(1, ordered, before_points, me + 1),
    ]
    to_before = [
        copy(2, samples_ref.at[pl.ds(0, edge)], after_samples, me - 1),
        copy(3, ordered, after_points, me - 1),
    ]

    @pl.when(has_after)
    def _():
        for c in to_after:
            c.start()

    @pl.when(has_before)
    def _():
        for c in to_before:
            c.start()

    def place_leaf(window_leaf, points, leaf, samples):
        for coord in range(3):
            rows[window_leaf, coord : coord + 1, :] = jnp.concatenate(
                [points[coord, leaf * lines + n : leaf * lines + n + 1, :] for n in range(lines)],
                axis=1,
            )
        high = samples.astype(jnp.bfloat16)
        low = (samples - high.astype(jnp.float32)).astype(jnp.bfloat16)
        pieces[window_leaf] = jnp.concatenate([high, low], axis=1)

    for leaf in range(leaves):
        place_leaf(
            HALO + leaf, ordered, leaf, samples_ref[leaf * leaf_size : (leaf + 1) * leaf_size, :]
        )
        for coord in range(3):
            for n in range(lines):
                wide = jnp.broadcast_to(
                    ordered[coord, leaf * lines + n : leaf * lines + n + 1, :], (128, 128)
                )
                columns[coord, leaf, n * 128 : (n + 1) * 128, :] = wide.T

    def tile_product(leaf, window_leaf, weight):
        others = rows[window_leaf]
        chunk = 64
        for start in range(0, leaf_size, chunk):
            distance = 0.0
            for coord in range(3):
                own = columns[coord, leaf, start : start + chunk, :]
                own = jnp.concatenate([own] * lines, axis=1)
                gap = own - others[coord : coord + 1, :]
                distance = distance + gap * gap
            value = jnp.exp(-SPREAD * distance)
            if weight is not None:
                value = value * weight
            high = value.astype(jnp.bfloat16)
            low = (value - high.astype(jnp.float32)).astype(jnp.bfloat16)
            tile[start : start + chunk, :] = high
            tile[leaf_size + start : leaf_size + start + chunk, :] = low
        product = lax.dot_general(
            tile[...],
            pieces[window_leaf],
            (((1,), (0,)), ((), ())),
            preferred_element_type=jnp.float32,
        )
        product = product[:leaf_size] + product[leaf_size:]
        return product[:, :rank] + product[:, rank:]

    @pl.loop(0, leaves)
    def _(leaf):
        sampled_ref[leaf] = tile_product(leaf, HALO + leaf, None)

    @pl.when(has_before)
    def _():
        copy(0, samples_ref.at[pl.ds(0, edge)], before_samples, me - 1).wait_recv()
        copy(1, ordered, before_points, me - 1).wait_recv()

    @pl.when(has_after)
    def _():
        copy(2, samples_ref.at[pl.ds(0, edge)], after_samples, me + 1).wait_recv()
        copy(3, ordered, after_points, me + 1).wait_recv()

    @pl.when(jnp.logical_not(has_before))
    def _():
        before_samples[...] = jnp.zeros_like(before_samples)
        before_points[...] = jnp.zeros_like(before_points)

    @pl.when(jnp.logical_not(has_after))
    def _():
        after_samples[...] = jnp.zeros_like(after_samples)
        after_points[...] = jnp.zeros_like(after_points)

    for h in range(HALO):
        part = slice(h * leaf_size, (h + 1) * leaf_size)
        place_leaf(h, before_points, leaves - HALO + h, before_samples[part, :])
        place_leaf(HALO + leaves + h, after_points, h, after_samples[part, :])

    @pl.loop(0, leaves)
    def _(leaf):
        total = sampled_ref[leaf]
        for k in range(MAXNB):
            weight = (count_ref[leaf] > k).astype(jnp.float32)
            total = total + tile_product(leaf, near_ref[leaf, k], weight)
        sampled_ref[leaf] = total
        gram_ref[leaf] = dot(total, total, 0, 0)

    @pl.when(has_after)
    def _():
        for c in to_after:
            c.wait_send()

    @pl.when(has_before)
    def _():
        for c in to_before:
            c.wait_send()


def sample_leaves(points, tree_order, samples, near_leaves, near_counts):
    leaves = near_counts.shape[0]
    rank = samples.shape[1]
    leaf_size = samples.shape[0] // leaves
    lines = points.shape[1] // 128
    window = leaves + 2 * HALO
    edge = HALO * leaf_size
    vmem = pl.BlockSpec(memory_space=pltpu.VMEM)
    smem = pl.BlockSpec(memory_space=pltpu.SMEM)
    block = (3, lines, 128)
    return pl.pallas_call(
        sample_kernel,
        out_shape=(
            jax.ShapeDtypeStruct((leaves, leaf_size, rank), jnp.float32),
            jax.ShapeDtypeStruct((leaves, rank, rank), jnp.float32),
        ),
        in_specs=[smem, smem, vmem, vmem, vmem],
        out_specs=(vmem, vmem),
        scratch_shapes=[
            pltpu.VMEM(block, jnp.float32),
            pltpu.VMEM(block, jnp.float32),
            pltpu.VMEM(block, jnp.float32),
            pltpu.VMEM((edge, rank), jnp.float32),
            pltpu.VMEM((edge, rank), jnp.float32),
            pltpu.VMEM((window, 8, leaf_size), jnp.float32),
            pltpu.VMEM((3, leaves, leaf_size, 128), jnp.float32),
            pltpu.VMEM((window, leaf_size, 2 * rank), jnp.bfloat16),
            pltpu.VMEM((2 * leaf_size, leaf_size), jnp.bfloat16),
            pltpu.SemaphoreType.DMA((4,)),
            pltpu.SemaphoreType.DMA((4,)),
        ],
        compiler_params=pltpu.CompilerParams(
            vmem_limit_bytes=40 * 2**20, collective_id=0, has_side_effects=True
        ),
        name="sample_leaves",
    )(
        near_leaves,
        near_counts,
        points.reshape(block),
        tree_order.reshape(lines, 128),
        samples,
    )


def eliminate(work, first, count):
    size = work.shape[-1]
    chunks = PANEL // 8
    lane = lax.broadcasted_iota(jnp.int32, (1, 1, size), 2)
    sub = lax.broadcasted_iota(jnp.int32, (1, 8, size), 1)
    group = pl.ds(first, count)
    for top in range(0, size, PANEL):
        parts = [work[group, top + 8 * t : top + 8 * t + 8, :] for t in range(chunks)]
        for k in range(PANEL):
            own, s = k // 8, k % 8
            here = lane == top + k
            columns = {
                t: jnp.broadcast_to(parts[t][:, :, top + k : top + k + 1], parts[t].shape)
                for t in range(own, chunks)
            }
            d = columns[own][:, s : s + 1, :]
            r = lax.rsqrt(d)
            r = r * (1.5 - 0.5 * d * r * r)
            row = jnp.where(here, r, parts[own][:, s : s + 1, :] * r)
            for t in range(own, chunks):
                new = jnp.where(here, 0.0, parts[t]) - (columns[t] * r) * row
                if t == own:
                    new = jnp.where(sub > s, new, jnp.where(sub == s, row, parts[t]))
                parts[t] = new
        for t in range(chunks):
            work[group, top + 8 * t : top + 8 * t + 8, :] = parts[t]
        below = top + PANEL
        if below < size:
            rows_id = lax.broadcasted_iota(jnp.int32, (PANEL, size), 0) + top
            lane2 = lax.broadcasted_iota(jnp.int32, (PANEL, size), 1)
            in_panel = (lane2 >= top) & (lane2 < below)
            for g in range(count):
                panel = work[first + g, top:below, :]
                left = panel.T[below:, :]
                right = jnp.where(in_panel & (lane2 > rows_id), 0.0, panel)
                lane3 = lax.broadcasted_iota(jnp.int32, (size - below, size), 1)
                old = work[first + g, below:, :]
                old = jnp.where((lane3 >= top) & (lane3 < below), 0.0, old)
                work[first + g, below:, :] = old - dot(left, right)


def split_factor(w):
    row = lax.broadcasted_iota(jnp.int32, w.shape, 0)
    column = lax.broadcasted_iota(jnp.int32, w.shape, 1)
    upper = jnp.where(row < column, w, jnp.where(row == column, 1.0 / w, 0.0))
    return upper, jnp.where(row >= column, w, 0.0)


def node_kernel(
    gram_ref, sampled_ref, leaf_ref, local_ref, upper_ref, root_ref,
    work, sums, partner_sums, factors, partner_factors,
    sum_send, sum_recv, factor_send, factor_recv,
):
    leaves = gram_ref.shape[0]
    nodes = 2 * leaves - 1
    rank = gram_ref.shape[-1]
    levels = upper_ref.shape[0]
    me = linear_position()

    def partner(level):
        return device_at(me + (1 - me // 2**level % 2 * 2) * 2**level)

    barrier = pltpu.get_barrier_semaphore()
    for level in range(levels):
        pl.semaphore_signal(
            barrier, inc=1, device_id=partner(level), device_id_type=pl.DeviceIdType.MESH
        )

    work[pl.ds(0, leaves)] = gram_ref[...]
    for node in range(leaves, nodes):
        child = 2 * (node - leaves)
        work[node] = work[child] + work[child + 1]
    sums[0] = work[nodes - 1]
    pl.semaphore_wait(barrier, levels)

    def copy(level, source, target, send, recv):
        return pltpu.make_async_remote_copy(
            src_ref=source.at[level],
            dst_ref=target.at[level],
            send_sem=send.at[level],
            recv_sem=recv.at[level],
            device_id=partner(level),
            device_id_type=pl.DeviceIdType.MESH,
        )

    sum_copies = [copy(h, sums, partner_sums, sum_send, sum_recv) for h in range(levels)]
    factor_copies = [
        copy(h, factors, partner_factors, factor_send, factor_recv) for h in range(levels)
    ]

    def climb(level):
        if level < levels:
            sum_copies[level].wait_recv()
            sums[level + 1] = sums[level] + partner_sums[level]
            if level + 1 < levels:
                sum_copies[level + 1].start()

    def leaf_basis(leaf):
        leaf_ref[leaf] = dot(sampled_ref[leaf], split_factor(work[leaf])[1], 1, 1)

    def node_basis(node):
        child = 2 * (node - leaves)
        inverse = split_factor(work[node])[1]
        for half in range(2):
            factor = split_factor(work[child + half])[0]
            local_ref[node - leaves, half * rank : (half + 1) * rank, :] = dot(
                factor, inverse, 1, 1
            )

    sum_copies[0].start()
    eliminate(work, 0, leaves)
    climb(0)
    for leaf in range(leaves // 2):
        leaf_basis(leaf)
    climb(1)
    for leaf in range(leaves // 2, leaves):
        leaf_basis(leaf)
    climb(2)
    eliminate(work, leaves, leaves - 1)
    climb(3)
    middle = leaves + leaves // 2
    for node in range(leaves, middle):
        node_basis(node)
    for level in range(4, levels):
        climb(level)
    factors[0] = work[nodes - 1]
    for level in range(1, levels + 1):
        factors[level] = sums[level]
    eliminate(factors, 1, levels)
    for c in factor_copies:
        c.start()
    root_ref[...] = split_factor(factors[levels])[0]
    for node in range(middle, nodes):
        node_basis(node)
    for level in range(levels):
        factor_copies[level].wait_recv()
        inverse = split_factor(factors[level + 1])[1]
        own = split_factor(factors[level])[0]
        other = split_factor(partner_factors[level])[0]
        second = me // 2**level % 2 == 1
        upper_ref[level, :rank, :] = dot(jnp.where(second, other, own), inverse, 1, 1)
        upper_ref[level, rank:, :] = dot(jnp.where(second, own, other), inverse, 1, 1)
    for c in sum_copies + factor_copies:
        c.wait_send()


def per_device(points, tree_order, samples, near_leaves, near_counts):
    leaves = near_counts.shape[0]
    rank_width = samples.shape[1]
    leaf_size = samples.shape[0] // leaves
    sampled, grams = sample_leaves(points, tree_order, samples, near_leaves, near_counts)

    devices = lax.axis_size("tx") * lax.axis_size("ty")
    levels = devices.bit_length() - 1
    matrix = (rank_width, rank_width)
    vmem = pl.BlockSpec(memory_space=pltpu.VMEM)
    leaf_basis, local_bases, upper_bases, root = pl.pallas_call(
        node_kernel,
        out_shape=(
            jax.ShapeDtypeStruct((leaves, leaf_size, rank_width), jnp.float32),
            jax.ShapeDtypeStruct((leaves - 1, 2 * rank_width, rank_width), jnp.float32),
            jax.ShapeDtypeStruct((levels, 2 * rank_width, rank_width), jnp.float32),
            jax.ShapeDtypeStruct(matrix, jnp.float32),
        ),
        in_specs=[vmem, vmem],
        out_specs=(vmem,) * 4,
        scratch_shapes=[
            pltpu.VMEM((2 * leaves - 1, *matrix), jnp.float32),
            pltpu.VMEM((levels + 1, *matrix), jnp.float32),
            pltpu.VMEM((levels, *matrix), jnp.float32),
            pltpu.VMEM((levels + 1, *matrix), jnp.float32),
            pltpu.VMEM((levels, *matrix), jnp.float32),
        ]
        + [pltpu.SemaphoreType.DMA((levels,))] * 4,
        compiler_params=pltpu.CompilerParams(
            vmem_limit_bytes=40 * 2**20, collective_id=1, has_side_effects=True
        ),
        name="tree_nodes",
    )(grams, sampled)
    return (leaf_basis.reshape(leaves * leaf_size, rank_width), local_bases, upper_bases, root)


def solution(mesh):
    return jax.shard_map(
        per_device,
        mesh=mesh,
        in_specs=(
            P(None, ("tx", "ty")),
            P(("tx", "ty"), None),
            P(("tx", "ty"), None),
            P(("tx", "ty"), None),
            P(("tx", "ty")),
        ),
        out_specs=(
            P(("tx", "ty"), None),
            P(("tx", "ty"), None, None),
            P(("tx", "ty"), None, None),
            P(),
        ),
        check_vma=False,
    )
```
